128 devices in a mesh: replica: 8 (over z, y_hi), fsdp: 2 (over y_lo), context: 8 (over x, core).
Axes of the slice: x: 4, y: 4 (y_hi: 2, y_lo: 2; y = y_hi * 2 + y_lo), z: 4, core: 2. Of those that a mesh axis runs over, the one named last changes fastest.
Arguments:
- queries: bfloat16 [8, 4096, 5120], P('replica', ('fsdp', 'context')), may hold values from -7 to 7
- keys: bfloat16 [8, 4096, 1024], P('replica', ('fsdp', 'context')), may hold values from -7 to 7
- values: bfloat16 [8, 4096, 1024], P('replica', ('fsdp', 'context')), may hold values from -6 to 6
- valid_length: int32 [8], P('replica'), may hold values from 2048 to 4096
- norm_gain: float32 [5120], replicated, may hold values from 0.1 to 1.9
- value_head: float32 [5120], replicated, may hold values from -0.078125 to 0.078125
- policy_in: bfloat16 [8, 4096, 1536], P('replica', ('fsdp', 'context')), may hold values from -6 to 6
- cotangent: bfloat16 [8, 4096, 2048], P('replica', ('fsdp', 'context')), may hold values from -6 to 6
- qkv_weight: bfloat16 [1536, 2048], P('fsdp'), may hold values from -0.125 to 0.125
Outputs:
- attn_out: bfloat16 [8, 4096, 5120], P('replica', ('fsdp', 'context'))
- advantage: float32 [8], P('replica')
- input_grad: bfloat16 [8, 4096, 1536], P('replica', ('fsdp', 'context'))
- weight_grad: float32 [1536, 2048], P('fsdp')
The draws below stay inside these ranges and needn't reach their ends.
All inputs are finite; a program needn't handle non-finite values.
Results may differ from the reference program's by a relative error of at most 0.018.
Values may be sent and summed in bfloat16 or wider, within the bound.
No kernel may reach another device: no remote copies, remote signals or barrier semaphores. Data moves between devices by JAX's collectives and lax.ppermute only.
A program may use at most 192 MiB of HBM per device.

```python
import math
import jax
import jax.numpy as jnp
from jax import lax

HEADS = 40
KV_HEADS = 8
HEAD_DIM = 128
D = 5120
P_D = 1536
P_QKV = 2048
SEQ = 4096
TRAJ = 8


def draw_queries(key, part):
    key = jax.random.fold_in(key, 11)
    base = jnp.clip(jax.random.normal(key, (TRAJ, SEQ, HEADS * HEAD_DIM), jnp.float32), -6.0, 6.0)
    return base.astype(jnp.bfloat16)


def draw_keys(key, part):
    key = jax.random.fold_in(key, 12)
    base = jnp.clip(jax.random.normal(key, (TRAJ, SEQ, KV_HEADS * HEAD_DIM), jnp.float32), -6.0, 6.0)
    return base.astype(jnp.bfloat16)


def draw_valid_length(key, part):
    key = jax.random.fold_in(key, 13)
    first, second = jax.random.split(key)
    cut = jax.random.randint(first, (TRAJ,), 0, SEQ // 2 + 1)
    lengths = SEQ - cut
    longest = jax.random.randint(second, (), 0, TRAJ)
    index = jnp.arange(TRAJ)
    lengths = jnp.where(index == longest, SEQ, lengths)
    lengths = jnp.where(index == (longest + 1) % TRAJ, SEQ - SEQ // 2, lengths)
    return lengths.astype(jnp.int32)


def shard_levels(stream_key, dims, cuts, smallest, high):
    loudness = 1.0
    for dim, blocks in cuts:
        steps = jax.random.uniform(jax.random.fold_in(jax.random.fold_in(stream_key, 6), dim), (blocks,), jnp.float32, smallest / len(cuts), high / len(cuts))
        loudness = loudness * jnp.repeat(jnp.exp(steps), dims[dim] // blocks).reshape((-1,) + (1,) * (len(dims) - 1 - dim))
    return loudness


def normal_values(rng, extent, spread, limit, shards=(), kind=jnp.bfloat16):
    gain = shard_levels(rng, extent, shards, -0.22, 0.18) if shards else 1.0
    values = jax.random.normal(rng, extent, jnp.float32) * spread * gain
    return jnp.minimum(jnp.maximum(values, -limit), limit).astype(kind)


def setup_inputs(seed: int = 0) -> dict:
    streams_of = jax.random.split(jax.random.key(seed), 10)
    return {
        "queries": draw_queries(jax.random.fold_in(streams_of[9], 71), 0),
        "keys": draw_keys(jax.random.fold_in(streams_of[9], 71), 0),
        "values": normal_values(streams_of[2], (TRAJ, SEQ, KV_HEADS * HEAD_DIM), 1.0, 6.0, ((0, 8), (1, 16))),
        "valid_length": draw_valid_length(jax.random.fold_in(streams_of[9], 71), 0),
        "norm_gain": jnp.clip(1.0 + 0.18 * jax.random.normal(streams_of[4], (D,), jnp.float32), 0.1, 1.9),
        "value_head": normal_values(streams_of[5], (D,), D ** -0.5, 0.078125, (), jnp.float32),
        "policy_in": normal_values(streams_of[6], (TRAJ, SEQ, P_D), 1.0, 6.0, ((0, 8), (1, 16))),
        "cotangent": normal_values(streams_of[7], (TRAJ, SEQ, P_QKV), 1.0, 6.0, ((0, 8), (1, 16))),
        "qkv_weight": normal_values(streams_of[8], (P_D, P_QKV), P_QKV ** -0.5, 0.125, ((0, 2),)),
    }


def attend_trajectory(args):
    query, key, value, length = args
    group = HEADS // KV_HEADS
    scale = 1.0 / math.sqrt(HEAD_DIM)
    block = 256 if SEQ % 256 == 0 else SEQ
    positions = jnp.arange(SEQ, dtype=jnp.int32)
    query_blocks = query.reshape(SEQ // block, block, KV_HEADS, group, HEAD_DIM)
    pos_blocks = positions.reshape(SEQ // block, block)
    key_heads = key.reshape(SEQ, KV_HEADS, HEAD_DIM).astype(jnp.float32)
    value_heads = value.reshape(SEQ, KV_HEADS, HEAD_DIM).astype(jnp.float32)

    def one_block(inner):
        q_block, q_pos = inner
        score = jnp.einsum('qkgd,skd->kgqs', q_block.astype(jnp.float32), key_heads) * scale
        allowed = (positions[None, :] <= q_pos[:, None]) & (positions[None, :] < length)
        score = jnp.where(allowed[None, None], score, -1e+30)
        top = lax.optimization_barrier(jnp.max(score, axis=-1, keepdims=True))
        weights = jnp.where(allowed[None, None], jnp.exp(score - top), 0.0)
        total = lax.optimization_barrier(jnp.sum(weights, axis=-1))
        weights_bf = lax.optimization_barrier(weights.astype(jnp.bfloat16))
        mixed = jnp.einsum('kgqs,skd->kgqd', weights_bf.astype(jnp.float32), value_heads)
        mixed = mixed / total[..., None]
        return jnp.transpose(mixed, (2, 0, 1, 3)).reshape(block, HEADS * HEAD_DIM)
    result = lax.map(one_block, (query_blocks, pos_blocks))
    return result.reshape(SEQ, HEADS * HEAD_DIM).astype(jnp.bfloat16)

def reference(queries, keys, values, valid_length, norm_gain, value_head, policy_in, cotangent, qkv_weight):
    attn_out = lax.map(attend_trajectory, (queries, keys, values, valid_length))
    outputs = attn_out.astype(jnp.float32)
    mean_sq = lax.optimization_barrier(jnp.mean(outputs * outputs, axis=-1, keepdims=True))
    normed = outputs * lax.rsqrt(mean_sq + 1e-06) * norm_gain
    score_tok = lax.optimization_barrier(jnp.sum(normed * value_head, axis=-1))
    positions = jnp.arange(SEQ, dtype=jnp.int32)
    valid = positions[None, :] < valid_length[:, None]
    lengths = valid_length.astype(jnp.float32)
    reward = lax.optimization_barrier(jnp.sum(jnp.where(valid, score_tok, 0.0), axis=1)) / jnp.sqrt(lengths)
    mean = jnp.mean(reward)
    var = jnp.mean(reward * reward) - mean * mean
    advantage = (reward - mean) / jnp.sqrt(var + 0.25)
    masked = jnp.where(valid[..., None], cotangent, jnp.zeros_like(cotangent))
    raw = jnp.dot(masked.reshape(TRAJ * SEQ, P_QKV), qkv_weight.T, preferred_element_type=jnp.float32)
    input_grad = (advantage[:, None, None] * raw.reshape(TRAJ, SEQ, P_D)).astype(jnp.bfloat16)

    def term(args):
        inputs, masked_rows = args
        return jnp.dot(inputs.T, masked_rows, preferred_element_type=jnp.float32)
    terms = lax.map(term, (policy_in, masked))
    weight_grad = lax.optimization_barrier(jnp.sum(advantage[:, None, None] * terms, axis=0))
    return (attn_out, advantage, input_grad, weight_grad)
```

```python
import math

import jax
import jax.numpy as jnp
from jax import lax
from jax.experimental import pallas as pl
from jax.experimental.pallas import tpu as pltpu
from jax.sharding import PartitionSpec as P

HEAD_DIM = 128
GROUP = 5
BLOCK = 512
HALF = BLOCK // 2
NEG = -1e30
FAR = 1 << 24
LOG2_SCALE = math.log2(math.e) / math.sqrt(HEAD_DIM)
BF = jnp.bfloat16
F32 = jnp.float32


VMEM_BYTES = 26 * 1024 * 1024
ANY = pl.BlockSpec(memory_space=pl.ANY)
PARAMS = pltpu.CompilerParams(vmem_limit_bytes=VMEM_BYTES)
TINY = pl.CostEstimate(flops=1, bytes_accessed=1, transcendentals=0)


def split_kv(info, keys, values):
    rows, half = keys.shape[0], keys.shape[1] // 2

    def kernel(info_ref, k_send, k_keep, v_send, v_keep, send_ref, keep_ref):
        send_ref[0], send_ref[1] = k_send[...], v_send[...]
        keep_ref[0], keep_ref[1] = k_keep[...], v_keep[...]

    there = pl.BlockSpec((rows, half), lambda i, info: (0, 1 - info[2]))
    here = pl.BlockSpec((rows, half), lambda i, info: (0, info[2]))
    whole = pl.BlockSpec((2, rows, half), lambda i, info: (0, 0, 0))
    shape = jax.ShapeDtypeStruct((2, rows, half), BF)
    return pl.pallas_call(
        kernel,
        grid_spec=pltpu.PrefetchScalarGridSpec(
            num_scalar_prefetch=1,
            grid=(1,),
            in_specs=[there, here, there, here],
            out_specs=(whole, whole),
        ),
        out_shape=(shape, shape),
        compiler_params=PARAMS,
        cost_estimate=TINY,
        name="split_kv",
    )(info, keys, keys, values, values)


def policy_terms(info, inputs, cotangent, after):
    rows, wide = inputs.shape
    half, step = cotangent.shape[1] // 2, 256

    def kernel(info_ref, in_ref, there_ref, here_ref, *refs):
        send_ref, keep_ref = refs[-2:]
        pos = info_ref[0] + lax.broadcasted_iota(jnp.int32, (rows, half), 0)
        for ref, out in ((there_ref, send_ref), (here_ref, keep_ref)):
            masked = jnp.where(pos < info_ref[1], ref[...], jnp.zeros((rows, half), BF))
            out[...] = lax.dot_general(
                in_ref[...], masked, (((0,), (0,)), ((), ())), preferred_element_type=F32
            ).astype(BF)

    out = pl.BlockSpec((step, half), lambda i, info: (i, 0))
    shape = jax.ShapeDtypeStruct((wide, half), BF)
    return pl.pallas_call(
        kernel,
        grid_spec=pltpu.PrefetchScalarGridSpec(
            num_scalar_prefetch=1,
            grid=(wide // step,),
            in_specs=[
                pl.BlockSpec((rows, step), lambda i, info: (0, i)),
                pl.BlockSpec((rows, half), lambda i, info: (0, 1 - info[2])),
                pl.BlockSpec((rows, half), lambda i, info: (0, info[2])),
            ]
            + [ANY] * len(after),
            out_specs=(out, out),
        ),
        out_shape=(shape, shape),
        compiler_params=PARAMS,
        cost_estimate=TINY,
        name="policy_terms",
    )(info, inputs, cotangent, cotangent, *after)


def combine(weights, terms):
    n, (rows, cols) = len(terms), terms[0].shape

    def kernel(w_ref, *refs):
        total = refs[0][...].astype(F32) * w_ref[0]
        for i in range(1, n):
            total += refs[i][...].astype(F32) * w_ref[i]
        refs[n][...] = total.astype(BF)

    step = rows // 4
    spec = pl.BlockSpec((step, cols), lambda i, w: (i, 0))
    return pl.pallas_call(
        kernel,
        grid_spec=pltpu.PrefetchScalarGridSpec(
            num_scalar_prefetch=1, grid=(rows // step,), in_specs=[spec] * n, out_specs=spec
        ),
        out_shape=jax.ShapeDtypeStruct((rows, cols), BF),
        compiler_params=PARAMS,
        cost_estimate=TINY,
        name="combine",
    )(weights, *terms)


def place(info, pieces):
    n, (rows, cols) = len(pieces), pieces[0].shape
    chips = n // 2

    def kernel(info_ref, *refs):
        for i in range(n):

            @pl.when(pl.program_id(0) == i)
            def _():
                refs[n][...] = refs[i][...].astype(F32)

    return pl.pallas_call(
        kernel,
        grid_spec=pltpu.PrefetchScalarGridSpec(
            num_scalar_prefetch=1,
            grid=(n,),
            in_specs=[pl.BlockSpec((rows, cols), lambda i, info: (0, 0))] * n,
            out_specs=pl.BlockSpec(
                (rows, cols), lambda i, info: (info[i // 2], lax.rem(info[chips] + i, 2))
            ),
        ),
        out_shape=jax.ShapeDtypeStruct((chips * rows, 2 * cols), F32),
        compiler_params=PARAMS,
        cost_estimate=TINY,
        name="place",
    )(info, *pieces)


def add(info, sums, rows, steps, after):
    cols = sums[0][0][0].shape[1]
    counts = [len(terms) for terms in sums]
    n = sum(counts)

    def kernel(info_ref, *refs):
        start = 0
        for out, count in zip(refs[len(refs) - len(sums) :], counts):
            total = refs[start][...].astype(F32)
            for ref in refs[start + 1 : start + count]:
                total += ref[...].astype(F32)
            start += count
            out[...] = total.astype(BF)

    def spec(at):
        return pl.BlockSpec((rows, cols), lambda i, info: (at(i, info), 0))

    flat = [term for terms in sums for term in terms]
    shape = jax.ShapeDtypeStruct((rows * steps, cols), BF)
    return pl.pallas_call(
        kernel,
        grid_spec=pltpu.PrefetchScalarGridSpec(
            num_scalar_prefetch=1,
            grid=(steps,),
            in_specs=[spec(at) for _, at in flat] + [ANY] * len(after),
            out_specs=[spec(lambda i, info: i)] * len(sums),
        ),
        out_shape=[shape] * len(sums),
        compiler_params=PARAMS,
        cost_estimate=TINY,
        name="add",
    )(info, *(array for array, _ in flat), *after)


def pick(info, array, block, at, after):
    def kernel(info_ref, in_ref, *refs):
        refs[-1][...] = in_ref[...]

    zero = (0,) * len(block)
    return pl.pallas_call(
        kernel,
        grid_spec=pltpu.PrefetchScalarGridSpec(
            num_scalar_prefetch=1,
            grid=(1,),
            in_specs=[pl.BlockSpec(block, lambda i, info: at(info))] + [ANY] * len(after),
            out_specs=pl.BlockSpec(block, lambda i, info: zero),
        ),
        out_shape=jax.ShapeDtypeStruct(block, array.dtype),
        compiler_params=PARAMS,
        cost_estimate=TINY,
        name="pick",
    )(info, array, *after)


def attend(info, q, heads, pieces, joined, state, last, after=()):
    n, n_after, first = len(pieces), len(after), not state
    wide = GROUP * HEAD_DIM

    def kernel(info_ref, here_ref, got_ref, *refs):
        kv_refs, refs = refs[: 2 * n], refs[2 * n :]
        if not first:
            acc_in, ml_in = refs[:2]
            refs = refs[2:]
        refs = refs[n_after:]
        out_a, out_b, q_s, k_s, v_s, acc_s, m_s = refs
        q_base, length, core = info_ref[0], info_ref[1], info_ref[2]
        for h in range(GROUP):
            cols = slice(h * HEAD_DIM, (h + 1) * HEAD_DIM)
            for part, ref in enumerate((here_ref, got_ref)):
                at = slice(part * HALF, (part + 1) * HALF)
                scaled = ref[:, cols].astype(F32) * LOG2_SCALE
                high = scaled.astype(BF)
                q_s[h, at, :HEAD_DIM] = high
                q_s[h, at, HEAD_DIM:] = (scaled - high.astype(F32)).astype(BF)
            if first:
                acc_s[h] = jnp.zeros((BLOCK, 2 * HEAD_DIM), F32)
                m_s[h] = jnp.full((BLOCK, HEAD_DIM), NEG, F32)
            else:
                acc_s[h, :, :HEAD_DIM] = acc_in[0, :, cols]
                m_s[h] = jnp.broadcast_to(ml_in[0, :, h : h + 1], (BLOCK, HEAD_DIM))
                acc_s[h, :, HEAD_DIM:] = jnp.broadcast_to(
                    ml_in[0, :, 8 + h : 9 + h], (BLOCK, HEAD_DIM)
                )
        for i in range(n):
            at = slice(i * BLOCK, (i + 1) * BLOCK)
            k_s[at, :HEAD_DIM] = kv_refs[2 * i][0]
            k_s[at, HEAD_DIM:] = kv_refs[2 * i][0]
            v_s[at, :HEAD_DIM] = kv_refs[2 * i + 1][0]
            v_s[at, HEAD_DIM:] = jnp.ones((BLOCK, HEAD_DIM), BF)

        def tiles(i, count, keep):
            keys = count * BLOCK
            at = pl.ds(pl.multiple_of(i * BLOCK, BLOCK), keys)
            kk, v1 = k_s[at, :], v_s[at, :]

            def scores(h):
                s = lax.dot_general(
                    q_s[h], kk, (((1,), (1,)), ((), ())), preferred_element_type=F32
                )
                return s if keep is None else jnp.where(keep, s, NEG)

            s = scores(0)
            for h in range(GROUP):
                later = scores(h + 1) if h + 1 < GROUP else None
                m_old = m_s[h]
                m_new = jnp.maximum(m_old, jnp.max(s, axis=1, keepdims=True))
                p = jnp.exp2(s - jnp.tile(m_new, (1, keys // HEAD_DIM)))
                pv = jnp.dot(p.astype(BF), v1, preferred_element_type=F32)
                m_s[h] = m_new
                acc_s[h] = acc_s[h] * jnp.tile(jnp.exp2(m_old - m_new), (1, 2)) + pv
                s = later

        far = info_ref[3]
        for i in range(1, joined):
            far = jnp.maximum(far, info_ref[3 + i])
        together = (far < q_base) & (far + BLOCK <= length)

        @pl.when(together)
        def _():
            tiles(0, joined, None)

        @pl.loop(0, n)
        def _(i):
            base = info_ref[3 + i]

            @pl.when((base <= q_base) & (base < length) & jnp.logical_not(together & (i < joined)))
            def _():
                row = lax.broadcasted_iota(jnp.int32, (BLOCK, BLOCK), 0)
                col = lax.broadcasted_iota(jnp.int32, (BLOCK, BLOCK), 1)
                row = q_base + ((row + HALF * core) & (BLOCK - 1))
                col = base + ((col + HALF * core) & (BLOCK - 1))
                tiles(i, 1, (col <= row) & (col < length))

        if last:
            for h in range(GROUP):
                cols = slice(h * HEAD_DIM, (h + 1) * HEAD_DIM)
                mixed = (acc_s[h, :, :HEAD_DIM] / acc_s[h, :, HEAD_DIM:]).astype(BF)
                out_a[:, cols] = mixed[:HALF]
                out_b[:, cols] = mixed[HALF:]
        else:
            lane = lax.broadcasted_iota(jnp.int32, (BLOCK, HEAD_DIM), 1)
            ml = jnp.zeros((BLOCK, HEAD_DIM), F32)
            for h in range(GROUP):
                out_a[0, :, h * HEAD_DIM : (h + 1) * HEAD_DIM] = acc_s[h, :, :HEAD_DIM]
                ml = jnp.where(lane == h, m_s[h], ml)
                ml = jnp.where(lane == 8 + h, acc_s[h, :, HEAD_DIM:], ml)
            out_b[0] = ml

    def kv_spec(index):
        return pl.BlockSpec((1, BLOCK, HEAD_DIM), lambda g, info: (index, 0, g))

    operands, kv_specs = [], []
    for k, v in pieces:
        operands += [k, v]
        kv_specs += [kv_spec(0), kv_spec(v.shape[0] - 1)]
    q_specs = [
        pl.BlockSpec((HALF, wide), lambda g, info: (0, info[2] * heads + g)),
        pl.BlockSpec((HALF, wide), lambda g, info: (0, g)),
    ]
    out_spec = pl.BlockSpec((HALF, wide), lambda g, info: (0, g))
    acc_spec = pl.BlockSpec((1, BLOCK, wide), lambda g, info: (g, 0, 0))
    ml_spec = pl.BlockSpec((1, BLOCK, HEAD_DIM), lambda g, info: (g, 0, 0))
    acc_shape = jax.ShapeDtypeStruct((heads, BLOCK, wide), F32)
    ml_shape = jax.ShapeDtypeStruct((heads, BLOCK, HEAD_DIM), F32)
    out_shape = jax.ShapeDtypeStruct((HALF, heads * wide), BF)
    count = n * heads * GROUP * BLOCK * BLOCK
    return pl.pallas_call(
        kernel,
        grid_spec=pltpu.PrefetchScalarGridSpec(
            num_scalar_prefetch=1,
            grid=(heads,),
            in_specs=q_specs
            + kv_specs
            + ([] if first else [acc_spec, ml_spec])
            + [ANY] * n_after,
            out_specs=(out_spec, out_spec) if last else (acc_spec, ml_spec),
            scratch_shapes=[
                pltpu.VMEM((GROUP, BLOCK, 2 * HEAD_DIM), BF),
                pltpu.VMEM((n * BLOCK, 2 * HEAD_DIM), BF),
                pltpu.VMEM((n * BLOCK, 2 * HEAD_DIM), BF),
                pltpu.VMEM((GROUP, BLOCK, 2 * HEAD_DIM), F32),
                pltpu.VMEM((GROUP, BLOCK, HEAD_DIM), F32),
            ],
        ),
        out_shape=(out_shape, out_shape) if last else (acc_shape, ml_shape),
        compiler_params=PARAMS,
        cost_estimate=pl.CostEstimate(
            flops=count * HEAD_DIM, bytes_accessed=1, transcendentals=0
        ),
        name="attend",
    )(info, *q, *operands, *state, *after)


def finish(info, own, other, gain, head, after):
    rows, half = own.shape

    def kernel(info_ref, own_ref, other_ref, gain_ref, head_ref, *refs):
        out_ref, sum_ref = refs[-2:]
        base, length, core = info_ref[0], info_ref[1], info_ref[2]
        squares = jnp.zeros((rows, 1), F32)
        score = jnp.zeros((rows, 1), F32)
        for ref, side in ((own_ref, core), (other_ref, 1 - core)):
            cols = pl.ds(pl.multiple_of(side * half, half), half)
            part = ref[...]
            out_ref[:, cols] = part
            part = part.astype(F32)
            squares += jnp.sum(part * part, axis=1, keepdims=True)
            score += jnp.sum(part * (gain_ref[:, cols] * head_ref[:, cols]), axis=1, keepdims=True)
        score = score * lax.rsqrt(squares / (2 * half) + 1e-6)
        pos = base + lax.broadcasted_iota(jnp.int32, (rows, 1), 0)
        score = jnp.where(pos < length, score, 0.0)
        sum_ref[...] = jnp.broadcast_to(jnp.sum(score, axis=0, keepdims=True), (8, HEAD_DIM))

    return pl.pallas_call(
        kernel,
        grid_spec=pltpu.PrefetchScalarGridSpec(
            num_scalar_prefetch=1,
            grid=(1,),
            in_specs=[
                pl.BlockSpec((rows, half), lambda g, _: (0, 0)),
                pl.BlockSpec((rows, half), lambda g, _: (0, 0)),
                pl.BlockSpec((1, 2 * half), lambda g, _: (0, 0)),
                pl.BlockSpec((1, 2 * half), lambda g, _: (0, 0)),
            ]
            + [ANY] * len(after),
            out_specs=(
                pl.BlockSpec((rows, 2 * half), lambda g, _: (0, 0)),
                pl.BlockSpec((8, HEAD_DIM), lambda g, _: (0, 0)),
            ),
        ),
        out_shape=(
            jax.ShapeDtypeStruct((rows, 2 * half), BF),
            jax.ShapeDtypeStruct((8, HEAD_DIM), F32),
        ),
        compiler_params=PARAMS,
        cost_estimate=TINY,
        name="finish",
    )(info, own, other, gain[None], head[None], *after)


def shards(
    queries, keys, values, valid_length, norm_gain, value_head, policy_in, cotangent, qkv_weight
):
    n_rep, n_fsdp, n_ctx = (lax.axis_size(a) for a in ("replica", "fsdp", "context"))
    n_x, n_z = n_ctx // 2, n_rep // 2
    f, ctx, rep = lax.axis_index("fsdp"), lax.axis_index("context"), lax.axis_index("replica")
    x, core = ctx // 2, ctx % 2
    length = valid_length[0]
    rows = queries.shape[1]

    swap = [(i, i ^ 1) for i in range(n_ctx)]

    def along_x(step, planes):
        return [
            (p * n_ctx + i, p * n_ctx + (i + 2 * step) % n_ctx)
            for p in planes
            for i in range(n_ctx)
        ]

    def move(array, step, planes):
        return lax.ppermute(array, ("fsdp", "context"), along_x(step, planes))

    def half_of(kv, which, after):
        return pick(tok_info, kv, (1,) + kv.shape[1:], lambda info: (which, 0, 0), after)

    def side(array, which, axis):
        size = array.shape[axis] // 2
        return lax.dynamic_slice_in_dim(array, which * size, size, axis)

    tok_base = (f * n_ctx + ctx) * rows
    tok_info = jnp.stack([tok_base, length, core, f, x]).astype(jnp.int32)

    tok_base = (f * n_ctx + ctx) * rows
    tok_info = jnp.stack([tok_base, length, core, f, x]).astype(jnp.int32)
    kv_heads = keys.shape[2] // HEAD_DIM // 2

    kv_send, kv_keep = split_kv(tok_info, keys[0], values[0])
    kv_own = jnp.concatenate([kv_keep, lax.ppermute(kv_send, "context", swap)], axis=1)
    p_send, p_keep = policy_terms(tok_info, policy_in[0], cotangent[0], (kv_keep,))
    q_here = queries[0]
    q_send = pick(
        tok_info, q_here, (rows, q_here.shape[1] // 2), lambda info: (0, 1 - info[2]), (p_send,)
    )
    q_got = lax.ppermute(q_send, "context", swap)

    both, later = range(n_fsdp), [1]
    cross = lax.ppermute(kv_own, "fsdp", [(0, 1)])
    ring_one, ring_three = move(kv_own, 1, both), move(kv_own, -1, both)
    cross_one, cross_three = move(cross, 1, later), move(cross, -1, later)

    pairs = []
    for r in range(n_rep):
        for g in range(n_fsdp):
            y_to = ((r % 2) * 2 + g) ^ 3
            pairs.append((r * 2 + g, ((r // 2) * 2 + y_to // 2) * 2 + y_to % 2))
    weight_other = lax.ppermute(qkv_weight, ("replica", "fsdp"), pairs)

    def pos(plane, d):
        return (plane * n_x + (x - d) % n_x) * BLOCK

    def near(*distances):
        return [pos(f, d) for d in distances]

    def other(*distances):
        return [jnp.where(f == 1, pos(0, d), FAR) for d in distances]

    def step(positions, pieces, joined, state, last=False, after=()):
        items = [pos(f, 0), length, core] + positions
        info = jnp.stack([jnp.asarray(i, jnp.int32) for i in items])
        return attend(info, (q_here, q_got), kv_heads, pieces, joined, state, last, after)

    chunk = p_keep.shape[0] // (n_fsdp * n_x)
    got = lax.ppermute(p_send, "context", swap)
    p_send, p_keep = add(
        tok_info,
        [
            [(a, lambda i, info: (1 - info[3]) * n_x + i) for a in (p_keep, got)],
            [(a, lambda i, info: info[3] * n_x + i) for a in (p_keep, got)],
        ],
        chunk,
        n_x,
        (cross,),
    )
    got = lax.ppermute(p_send, "fsdp", [(0, 1), (1, 0)])

    far = half_of(ring_one, 0, ()), half_of(ring_three, 1, ())
    ring_two = move(far[0], 1, both), move(far[1], -1, both)
    state = step(
        other(0) + near(1, 0),
        [(cross, cross), (ring_one, ring_one), (kv_own, kv_own)],
        2,
        (),
        after=(p_send,) + far,
    )
    far = half_of(cross_one, 0, state[1:]), half_of(cross_three, 1, state[1:])
    cross_two = move(far[0], 1, later), move(far[1], -1, later)
    state = step(near(3, 2), [(ring_three, ring_three), ring_two], 2, state, after=far)
    chunks = add(
        tok_info,
        [
            [(a, lambda i, info, d=d: lax.rem(info[4] + d, n_x)) for a in (p_keep, got)]
            for d in range(n_x)
        ],
        chunk,
        1,
        state[1:],
    )
    mixed = step(
        other(1, 3, 2),
        [(cross_one, cross_one), (cross_three, cross_three), cross_two],
        3,
        state,
        last=True,
        after=(chunks[0],),
    )
    parts = [chunks[0]] + [move(chunks[d], d, both) for d in range(1, n_x)]
    (total,) = add(tok_info, [[(a, lambda i, info: 0) for a in parts]], chunk, 1, mixed[:1])
    attn_out, reward_sum = finish(
        tok_info,
        mixed[0],
        lax.ppermute(mixed[1], "context", swap),
        norm_gain,
        value_head,
        (weight_other,),
    )

    valid = tok_base + jnp.arange(rows, dtype=jnp.int32) < length
    masked = jnp.where(valid[:, None], cotangent[0], jnp.zeros_like(cotangent[0]))

    z, y_hi = rep // 2, rep % 2
    def along_z(dz):
        return [(r, (r + 2 * dz) % n_rep) for r in range(n_rep)]

    beside = lax.ppermute(total, "replica", [(r, r ^ 1) for r in range(n_rep)])
    terms = []
    for dy, own in ((0, total), (1, beside)):
        for dz in range(n_z):
            source = ((z - dz) % n_z) * 2 + (y_hi ^ dy)
            terms.append((source, lax.ppermute(own, "replica", along_z(dz)) if dz else own))

    def raw(weight):
        return lax.dot_general(
            masked, weight, (((1,), (1,)), ((), ())), preferred_element_type=F32
        )

    raw_own, raw_other = raw(qkv_weight), raw(weight_other)

    partial = reward_sum[:1] / jnp.sqrt(length.astype(F32))
    n_dev = n_rep * n_fsdp * n_ctx
    sums = lax.all_to_all(
        jnp.broadcast_to(partial, (n_dev, HEAD_DIM)),
        ("replica", "fsdp", "context"),
        0,
        0,
        tiled=True,
    )
    reward = jnp.sum(sums[:, 0].reshape(n_rep, n_fsdp * n_ctx), axis=1)
    mean = jnp.mean(reward)
    var = jnp.mean(reward * reward) - mean * mean
    advantages = (reward - mean) / jnp.sqrt(var + 0.25)
    advantage = lax.dynamic_slice_in_dim(advantages, rep, 1)

    sources = jnp.stack([source for source, _ in terms])
    weight_rows = combine(advantages[sources], [one for _, one in terms])
    parts = []
    for d in (0, 1, 3, 2):
        part = move(weight_rows, d, both) if d else weight_rows
        parts += [part, lax.ppermute(part, "context", swap)]
    chips = [(x - d) % n_x for d in (0, 1, 3, 2)]
    weight_grad = place(jnp.stack(chips + [core]).astype(jnp.int32), parts)
    input_grad = jnp.where(
        f == 0,
        jnp.concatenate([raw_own, raw_other], axis=1),
        jnp.concatenate([raw_other, raw_own], axis=1),
    )
    input_grad = (advantage * input_grad).astype(BF)
    return (attn_out[None], advantage, input_grad[None], weight_grad)


def solution(mesh):
    tokens = P("replica", ("fsdp", "context"), None)
    in_specs = (tokens, tokens, tokens, P("replica"), P(), P(), tokens, tokens, P("fsdp", None))
    out_specs = (tokens, P("replica"), tokens, P("fsdp", None))
    return jax.shard_map(shards, mesh=mesh, in_specs=in_specs, out_specs=out_specs, check_vma=False)
```

```python
import math

import jax
import jax.numpy as jnp
from jax import lax
from jax.experimental import pallas as pl
from jax.experimental.pallas import tpu as pltpu
from jax.sharding import PartitionSpec as P

HEAD_DIM = 128
GROUP = 5
BLOCK = 512
HALF = BLOCK // 2
NEG = -1e30
FAR = 1 << 24
LOG2_SCALE = math.log2(math.e) / math.sqrt(HEAD_DIM)
BF = jnp.bfloat16
F32 = jnp.float32


VMEM_BYTES = 36 * 1024 * 1024
ANY = pl.BlockSpec(memory_space=pl.ANY)
PARAMS = pltpu.CompilerParams(vmem_limit_bytes=VMEM_BYTES)
TINY = pl.CostEstimate(flops=1, bytes_accessed=1, transcendentals=0)


def split_kv(info, keys, values):
    rows, half = keys.shape[0], keys.shape[1] // 2

    def kernel(info_ref, k_send, k_keep, v_send, v_keep, send_ref, keep_ref):
        send_ref[0], send_ref[1] = k_send[...], v_send[...]
        keep_ref[0], keep_ref[1] = k_keep[...], v_keep[...]

    there = pl.BlockSpec((rows, half), lambda i, info: (0, 1 - info[2]))
    here = pl.BlockSpec((rows, half), lambda i, info: (0, info[2]))
    whole = pl.BlockSpec((2, rows, half), lambda i, info: (0, 0, 0))
    shape = jax.ShapeDtypeStruct((2, rows, half), BF)
    return pl.pallas_call(
        kernel,
        grid_spec=pltpu.PrefetchScalarGridSpec(
            num_scalar_prefetch=1,
            grid=(1,),
            in_specs=[there, here, there, here],
            out_specs=(whole, whole),
        ),
        out_shape=(shape, shape),
        compiler_params=PARAMS,
        cost_estimate=TINY,
        name="split_kv",
    )(info, keys, keys, values, values)


def policy_terms(info, inputs, cotangent, after):
    rows, wide = inputs.shape
    half, step = cotangent.shape[1] // 2, 256

    def kernel(info_ref, in_ref, there_ref, here_ref, *refs):
        send_ref, keep_ref = refs[-2:]
        pos = info_ref[0] + lax.broadcasted_iota(jnp.int32, (rows, half), 0)
        for ref, out in ((there_ref, send_ref), (here_ref, keep_ref)):
            masked = jnp.where(pos < info_ref[1], ref[...], jnp.zeros((rows, half), BF))
            out[...] = lax.dot_general(
                in_ref[...], masked, (((0,), (0,)), ((), ())), preferred_element_type=F32
            ).astype(BF)

    out = pl.BlockSpec((step, half), lambda i, info: (i, 0))
    shape = jax.ShapeDtypeStruct((wide, half), BF)
    return pl.pallas_call(
        kernel,
        grid_spec=pltpu.PrefetchScalarGridSpec(
            num_scalar_prefetch=1,
            grid=(wide // step,),
            in_specs=[
                pl.BlockSpec((rows, step), lambda i, info: (0, i)),
                pl.BlockSpec((rows, half), lambda i, info: (0, 1 - info[2])),
                pl.BlockSpec((rows, half), lambda i, info: (0, info[2])),
            ]
            + [ANY] * len(after),
            out_specs=(out, out),
        ),
        out_shape=(shape, shape),
        compiler_params=PARAMS,
        cost_estimate=TINY,
        name="policy_terms",
    )(info, inputs, cotangent, cotangent, *after)


def combine(weights, terms, after):
    n, (rows, cols) = len(terms), terms[0].shape

    def kernel(w_ref, *refs):
        total = refs[0][...].astype(F32) * w_ref[0]
        for i in range(1, n):
            total += refs[i][...].astype(F32) * w_ref[i]
        refs[-1][...] = total.astype(BF)

    step = rows // 4
    spec = pl.BlockSpec((step, cols), lambda i, w: (i, 0))
    return pl.pallas_call(
        kernel,
        grid_spec=pltpu.PrefetchScalarGridSpec(
            num_scalar_prefetch=1,
            grid=(rows // step,),
            in_specs=[spec] * n + [ANY] * len(after),
            out_specs=spec,
        ),
        out_shape=jax.ShapeDtypeStruct((rows, cols), BF),
        compiler_params=PARAMS,
        cost_estimate=TINY,
        name="combine",
    )(weights, *terms, *after)


def place(info, pieces):
    n, (rows, cols) = len(pieces), pieces[0].shape
    chips = n // 2

    def kernel(info_ref, *refs):
        for i in range(n):

            @pl.when(pl.program_id(0) == i)
            def _():
                refs[n][...] = refs[i][...].astype(F32)

    return pl.pallas_call(
        kernel,
        grid_spec=pltpu.PrefetchScalarGridSpec(
            num_scalar_prefetch=1,
            grid=(n,),
            in_specs=[pl.BlockSpec((rows, cols), lambda i, info: (0, 0))] * n,
            out_specs=pl.BlockSpec(
                (rows, cols), lambda i, info: (info[i // 2], lax.rem(info[chips] + i, 2))
            ),
        ),
        out_shape=jax.ShapeDtypeStruct((chips * rows, 2 * cols), F32),
        compiler_params=PARAMS,
        cost_estimate=TINY,
        name="place",
    )(info, *pieces)


def add(info, sums, rows, steps, after):
    cols = sums[0][0][0].shape[1]
    counts = [len(terms) for terms in sums]
    n = sum(counts)

    def kernel(info_ref, *refs):
        start = 0
        for out, count in zip(refs[len(refs) - len(sums) :], counts):
            total = refs[start][...].astype(F32)
            for ref in refs[start + 1 : start + count]:
                total += ref[...].astype(F32)
            start += count
            out[...] = total.astype(BF)

    def spec(at):
        return pl.BlockSpec((rows, cols), lambda i, info: (at(i, info), 0))

    flat = [term for terms in sums for term in terms]
    shape = jax.ShapeDtypeStruct((rows * steps, cols), BF)
    return pl.pallas_call(
        kernel,
        grid_spec=pltpu.PrefetchScalarGridSpec(
            num_scalar_prefetch=1,
            grid=(steps,),
            in_specs=[spec(at) for _, at in flat] + [ANY] * len(after),
            out_specs=[spec(lambda i, info: i)] * len(sums),
        ),
        out_shape=[shape] * len(sums),
        compiler_params=PARAMS,
        cost_estimate=TINY,
        name="add",
    )(info, *(array for array, _ in flat), *after)


def pick(info, array, block, at, after):
    def kernel(info_ref, in_ref, *refs):
        refs[-1][...] = in_ref[...]

    zero = (0,) * len(block)
    return pl.pallas_call(
        kernel,
        grid_spec=pltpu.PrefetchScalarGridSpec(
            num_scalar_prefetch=1,
            grid=(1,),
            in_specs=[pl.BlockSpec(block, lambda i, info: at(info))] + [ANY] * len(after),
            out_specs=pl.BlockSpec(block, lambda i, info: zero),
        ),
        out_shape=jax.ShapeDtypeStruct(block, array.dtype),
        compiler_params=PARAMS,
        cost_estimate=TINY,
        name="pick",
    )(info, array, *after)


def in_hbm(array):
    return pltpu.with_memory_space_constraint(array, pltpu.HBM)


def attend(info, q, heads, pieces, joined, state, last, flops, after=()):
    n, n_after, first = len(pieces), len(after), not state
    wide = GROUP * HEAD_DIM

    def kernel(info_ref, here_ref, got_ref, *refs):
        kv_refs, refs = refs[: 2 * n], refs[2 * n :]
        if not first:
            acc_in, ml_in = refs[:2]
            refs = refs[2:]
        refs = refs[n_after:]
        out_a, out_b, q_s, k_s, v_s, acc_s, m_s = refs
        q_base, length, core = info_ref[0], info_ref[1], info_ref[2]
        for h in range(GROUP):
            cols = slice(h * HEAD_DIM, (h + 1) * HEAD_DIM)
            for part, ref in enumerate((here_ref, got_ref)):
                at = slice(part * HALF, (part + 1) * HALF)
                scaled = ref[:, cols].astype(F32) * LOG2_SCALE
                high = scaled.astype(BF)
                q_s[h, at, :HEAD_DIM] = high
                q_s[h, at, HEAD_DIM:] = (scaled - high.astype(F32)).astype(BF)
            if first:
                acc_s[h] = jnp.zeros((BLOCK, 2 * HEAD_DIM), F32)
                m_s[h] = jnp.full((BLOCK, HEAD_DIM), NEG, F32)
            else:
                acc_s[h, :, :HEAD_DIM] = acc_in[0, :, cols]
                m_s[h] = jnp.broadcast_to(ml_in[0, :, h : h + 1], (BLOCK, HEAD_DIM))
                acc_s[h, :, HEAD_DIM:] = jnp.broadcast_to(
                    ml_in[0, :, 8 + h : 9 + h], (BLOCK, HEAD_DIM)
                )
        for i in range(n):
            at = slice(i * BLOCK, (i + 1) * BLOCK)
            k_s[at, :HEAD_DIM] = kv_refs[2 * i][0]
            k_s[at, HEAD_DIM:] = kv_refs[2 * i][0]
            v_s[at, :HEAD_DIM] = kv_refs[2 * i + 1][0]
            v_s[at, HEAD_DIM:] = jnp.ones((BLOCK, HEAD_DIM), BF)

        def tiles(i, count, keep):
            keys = count * BLOCK
            at = pl.ds(pl.multiple_of(i * BLOCK, BLOCK), keys)
            kk, v1 = k_s[at, :], v_s[at, :]

            def scores(h):
                s = lax.dot_general(
                    q_s[h], kk, (((1,), (1,)), ((), ())), preferred_element_type=F32
                )
                return s if keep is None else jnp.where(keep, s, NEG)

            s = scores(0)
            for h in range(GROUP):
                later = scores(h + 1) if h + 1 < GROUP else None
                m_old = m_s[h]
                m_new = jnp.maximum(m_old, jnp.max(s, axis=1, keepdims=True))
                p = jnp.exp2(s - jnp.tile(m_new, (1, keys // HEAD_DIM)))
                pv = jnp.dot(p.astype(BF), v1, preferred_element_type=F32)
                m_s[h] = m_new
                acc_s[h] = acc_s[h] * jnp.tile(jnp.exp2(m_old - m_new), (1, 2)) + pv
                s = later

        taken = []
        for begin, count in joined:
            far = info_ref[3 + begin]
            for i in range(begin + 1, begin + count):
                far = jnp.maximum(far, info_ref[3 + i])
            together = (far < q_base) & (far + BLOCK <= length)
            taken.append((begin, count, together))

            @pl.when(together)
            def _():
                tiles(begin, count, None)

        @pl.loop(0, n)
        def _(i):
            base = info_ref[3 + i]
            use = (base <= q_base) & (base < length)
            for begin, count, together in taken:
                use &= jnp.logical_not(together & (i >= begin) & (i < begin + count))

            @pl.when(use)
            def _():
                row = lax.broadcasted_iota(jnp.int32, (BLOCK, BLOCK), 0)
                col = lax.broadcasted_iota(jnp.int32, (BLOCK, BLOCK), 1)
                row = q_base + ((row + HALF * core) & (BLOCK - 1))
                col = base + ((col + HALF * core) & (BLOCK - 1))
                tiles(i, 1, (col <= row) & (col < length))

        if last:
            for h in range(GROUP):
                cols = slice(h * HEAD_DIM, (h + 1) * HEAD_DIM)
                mixed = (acc_s[h, :, :HEAD_DIM] / acc_s[h, :, HEAD_DIM:]).astype(BF)
                out_a[:, cols] = mixed[:HALF]
                out_b[:, cols] = mixed[HALF:]
        else:
            lane = lax.broadcasted_iota(jnp.int32, (BLOCK, HEAD_DIM), 1)
            ml = jnp.zeros((BLOCK, HEAD_DIM), F32)
            for h in range(GROUP):
                out_a[0, :, h * HEAD_DIM : (h + 1) * HEAD_DIM] = acc_s[h, :, :HEAD_DIM]
                ml = jnp.where(lane == h, m_s[h], ml)
                ml = jnp.where(lane == 8 + h, acc_s[h, :, HEAD_DIM:], ml)
            out_b[0] = ml

    def kv_spec(index):
        return pl.BlockSpec((1, BLOCK, HEAD_DIM), lambda g, info: (index, 0, g))

    operands, kv_specs = [], []
    for kv in pieces:
        operands += [in_hbm(kv)] * 2
        kv_specs += [kv_spec(0), kv_spec(1)]
    q_specs = [
        pl.BlockSpec((HALF, wide), lambda g, info: (0, info[2] * heads + g)),
        pl.BlockSpec((HALF, wide), lambda g, info: (0, g)),
    ]
    out_spec = pl.BlockSpec((HALF, wide), lambda g, info: (0, g))
    acc_spec = pl.BlockSpec((1, BLOCK, wide), lambda g, info: (g, 0, 0))
    ml_spec = pl.BlockSpec((1, BLOCK, HEAD_DIM), lambda g, info: (g, 0, 0))
    acc_shape = pltpu.HBM((heads, BLOCK, wide), F32)
    ml_shape = pltpu.HBM((heads, BLOCK, HEAD_DIM), F32)
    out_shape = jax.ShapeDtypeStruct((HALF, heads * wide), BF)
    return pl.pallas_call(
        kernel,
        grid_spec=pltpu.PrefetchScalarGridSpec(
            num_scalar_prefetch=1,
            grid=(heads,),
            in_specs=q_specs
            + kv_specs
            + ([] if first else [acc_spec, ml_spec])
            + [ANY] * n_after,
            out_specs=(out_spec, out_spec) if last else (acc_spec, ml_spec),
            scratch_shapes=[
                pltpu.VMEM((GROUP, BLOCK, 2 * HEAD_DIM), BF),
                pltpu.VMEM((n * BLOCK, 2 * HEAD_DIM), BF),
                pltpu.VMEM((n * BLOCK, 2 * HEAD_DIM), BF),
                pltpu.VMEM((GROUP, BLOCK, 2 * HEAD_DIM), F32),
                pltpu.VMEM((GROUP, BLOCK, HEAD_DIM), F32),
            ],
        ),
        out_shape=(out_shape, out_shape) if last else (acc_shape, ml_shape),
        compiler_params=PARAMS,
        cost_estimate=pl.CostEstimate(
            flops=flops, bytes_accessed=1, transcendentals=0
        ),
        name="attend",
    )(info, *(in_hbm(a) for a in q), *operands, *(in_hbm(a) for a in state), *after)


def finish(info, own, other, gain, head, after):
    rows, half = own.shape

    def kernel(info_ref, own_ref, other_ref, gain_ref, head_ref, *refs):
        out_ref, sum_ref = refs[-2:]
        base, length, core = info_ref[0], info_ref[1], info_ref[2]
        squares = jnp.zeros((rows, 1), F32)
        score = jnp.zeros((rows, 1), F32)
        for ref, side in ((own_ref, core), (other_ref, 1 - core)):
            cols = pl.ds(pl.multiple_of(side * half, half), half)
            part = ref[...]
            out_ref[:, cols] = part
            part = part.astype(F32)
            squares += jnp.sum(part * part, axis=1, keepdims=True)
            score += jnp.sum(part * (gain_ref[:, cols] * head_ref[:, cols]), axis=1, keepdims=True)
        score = score * lax.rsqrt(squares / (2 * half) + 1e-6)
        pos = base + lax.broadcasted_iota(jnp.int32, (rows, 1), 0)
        score = jnp.where(pos < length, score, 0.0)
        sum_ref[...] = jnp.broadcast_to(jnp.sum(score, axis=0, keepdims=True), (8, HEAD_DIM))

    return pl.pallas_call(
        kernel,
        grid_spec=pltpu.PrefetchScalarGridSpec(
            num_scalar_prefetch=1,
            grid=(1,),
            in_specs=[
                pl.BlockSpec((rows, half), lambda g, _: (0, 0)),
                pl.BlockSpec((rows, half), lambda g, _: (0, 0)),
                pl.BlockSpec((1, 2 * half), lambda g, _: (0, 0)),
                pl.BlockSpec((1, 2 * half), lambda g, _: (0, 0)),
            ]
            + [ANY] * len(after),
            out_specs=(
                pl.BlockSpec((rows, 2 * half), lambda g, _: (0, 0)),
                pl.BlockSpec((8, HEAD_DIM), lambda g, _: (0, 0)),
            ),
        ),
        out_shape=(
            jax.ShapeDtypeStruct((rows, 2 * half), BF),
            jax.ShapeDtypeStruct((8, HEAD_DIM), F32),
        ),
        compiler_params=PARAMS,
        cost_estimate=TINY,
        name="finish",
    )(info, own, other, gain[None], head[None], *after)


def shards(
    queries, keys, values, valid_length, norm_gain, value_head, policy_in, cotangent, qkv_weight
):
    n_rep, n_fsdp, n_ctx = (lax.axis_size(a) for a in ("replica", "fsdp", "context"))
    n_x, n_z = n_ctx // 2, n_rep // 2
    f, ctx, rep = lax.axis_index("fsdp"), lax.axis_index("context"), lax.axis_index("replica")
    x, core = ctx // 2, ctx % 2
    length = valid_length[0]
    rows = queries.shape[1]

    swap = [(i, i ^ 1) for i in range(n_ctx)]

    def along_x(step, planes):
        return [
            (p * n_ctx + i, p * n_ctx + (i + 2 * step) % n_ctx)
            for p in planes
            for i in range(n_ctx)
        ]

    def move(array, step, planes):
        return lax.ppermute(array, ("fsdp", "context"), along_x(step, planes))

    def side(array, which, axis):
        size = array.shape[axis] // 2
        return lax.dynamic_slice_in_dim(array, which * size, size, axis)

    tok_base = (f * n_ctx + ctx) * rows
    tok_info = jnp.stack([tok_base, length, core, f, x]).astype(jnp.int32)

    tok_base = (f * n_ctx + ctx) * rows
    tok_info = jnp.stack([tok_base, length, core, f, x]).astype(jnp.int32)
    kv_heads = keys.shape[2] // HEAD_DIM // 2

    kv_send, kv_keep = split_kv(tok_info, keys[0], values[0])
    kv_own = jnp.concatenate([kv_keep, lax.ppermute(kv_send, "context", swap)], axis=1)
    p_send, p_keep = policy_terms(tok_info, policy_in[0], cotangent[0], (kv_keep,))
    q_here = queries[0]
    q_send = pick(
        tok_info, q_here, (rows, q_here.shape[1] // 2), lambda info: (0, 1 - info[2]), (p_send,)
    )
    q_got = lax.ppermute(q_send, "context", swap)

    both, later = range(n_fsdp), [1]
    cross = {0: lax.ppermute(kv_own, "fsdp", [(0, 1)])}
    ring = {d: move(kv_own, d, both) for d in (1, 3, 2)}
    for d in (1, 3, 2):
        cross[d] = move(cross[0], d, later)

    pairs = []
    for r in range(n_rep):
        for g in range(n_fsdp):
            y_to = ((r % 2) * 2 + g) ^ 3
            pairs.append((r * 2 + g, ((r // 2) * 2 + y_to // 2) * 2 + y_to % 2))
    weight_other = lax.ppermute(qkv_weight, ("replica", "fsdp"), pairs)

    def pos(plane, d):
        return (plane * n_x + (x - d) % n_x) * BLOCK

    def near(*distances):
        return [pos(f, d) for d in distances]

    def other(*distances):
        return [jnp.where(f == 1, pos(0, d), FAR) for d in distances]

    def step(positions, pieces, joined, state, flops, after):
        items = [pos(f, 0), length, core] + positions
        info = jnp.stack([jnp.asarray(i, jnp.int32) for i in items])
        return attend(info, (q_here, q_got), kv_heads, pieces, joined, state, bool(state), flops, after)

    chunk = p_keep.shape[0] // (n_fsdp * n_x)
    got = lax.ppermute(p_send, "context", swap)
    p_send, p_keep = add(
        tok_info,
        [
            [(a, lambda i, info: (1 - info[3]) * n_x + i) for a in (p_keep, got)],
            [(a, lambda i, info: info[3] * n_x + i) for a in (p_keep, got)],
        ],
        chunk,
        n_x,
        (cross[0],),
    )
    got = lax.ppermute(p_send, "fsdp", [(0, 1), (1, 0)])

    state = step(
        other(0) + near(1, 3, 2, 0),
        [cross[0], ring[1], ring[3], ring[2], kv_own],
        [(0, 2), (2, 2)],
        (),
        flops=24 * 10**9,
        after=(p_send,),
    )
    chunks = add(
        tok_info,
        [
            [(a, lambda i, info, d=d: lax.rem(info[4] + d, n_x)) for a in (p_keep, got)]
            for d in range(n_x)
        ],
        chunk,
        1,
        state[1:],
    )
    parts = [chunks[0]] + [move(chunks[d], d, both) for d in range(1, n_x)]
    mixed = step(
        other(1, 3, 2),
        [cross[1], cross[3], cross[2]],
        [(0, 3)],
        state,
        flops=24 * 10**9,
        after=(chunks[0],),
    )
    (total,) = add(tok_info, [[(a, lambda i, info: 0) for a in parts]], chunk, 1, mixed[:1])
    mixed_there = pick(tok_info, mixed[1], mixed[1].shape, lambda info: (0, 0), (total,))

    z, y_hi = rep // 2, rep % 2

    def along_z(array, dz):
        pairs = [(r, (r + 2 * dz) % n_rep) for r in range(n_rep)]
        return lax.ppermute(array, "replica", pairs) if dz else array

    terms = [along_z(total, dz) for dz in range(n_z)]
    sources = jnp.stack([((z - dz) % n_z) * 2 + y_hi for dz in range(n_z)])
    attn_out, reward_sum = finish(
        tok_info,
        mixed[0],
        lax.ppermute(mixed_there, "context", swap),
        norm_gain,
        value_head,
        (weight_other,),
    )

    valid = tok_base + jnp.arange(rows, dtype=jnp.int32) < length
    masked = jnp.where(valid[:, None], cotangent[0], jnp.zeros_like(cotangent[0]))

    def raw(weight):
        return lax.dot_general(
            masked, weight, (((1,), (1,)), ((), ())), preferred_element_type=F32
        )

    raw_own, raw_other = raw(qkv_weight), raw(weight_other)

    partial = reward_sum[:1] / jnp.sqrt(length.astype(F32))
    n_dev = n_rep * n_fsdp * n_ctx
    sums = lax.all_to_all(
        jnp.broadcast_to(partial, (n_dev, HEAD_DIM)),
        ("replica", "fsdp", "context"),
        0,
        0,
        tiled=True,
    )
    reward = jnp.sum(sums[:, 0].reshape(n_rep, n_fsdp * n_ctx), axis=1)
    mean = jnp.mean(reward)
    var = jnp.mean(reward * reward) - mean * mean
    advantages = (reward - mean) / jnp.sqrt(var + 0.25)
    advantage = lax.dynamic_slice_in_dim(advantages, rep, 1)

    weight_rows = combine(advantages[sources], terms, (raw_own, raw_other))
    beside = lax.ppermute(weight_rows, "replica", [(r, r ^ 1) for r in range(n_rep)])
    (weight_rows,) = add(
        tok_info, [[(a, lambda i, info: 0) for a in (weight_rows, beside)]], chunk, 1, ()
    )
    parts = []
    for d in (0, 1, 3, 2):
        part = move(weight_rows, d, both) if d else weight_rows
        parts += [part, lax.ppermute(part, "context", swap)]
    chips = [(x - d) % n_x for d in (0, 1, 3, 2)]
    weight_grad = place(jnp.stack(chips + [core]).astype(jnp.int32), parts)
    input_grad = jnp.where(
        f == 0,
        jnp.concatenate([raw_own, raw_other], axis=1),
        jnp.concatenate([raw_other, raw_own], axis=1),
    )
    input_grad = (advantage * input_grad).astype(BF)
    return (attn_out[None], advantage, input_grad[None], weight_grad)


def solution(mesh):
    tokens = P("replica", ("fsdp", "context"), None)
    in_specs = (tokens, tokens, tokens, P("replica"), P(), P(), tokens, tokens, P("fsdp", None))
    out_specs = (tokens, P("replica"), tokens, P("fsdp", None))
    return jax.shard_map(shards, mesh=mesh, in_specs=in_specs, out_specs=out_specs, check_vma=False)
```

```python
import math

import jax
import jax.numpy as jnp
from jax import lax
from jax.experimental import pallas as pl
from jax.experimental.pallas import tpu as pltpu
from jax.sharding import PartitionSpec as P

HEAD_DIM = 128
GROUP = 5
BLOCK = 512
HALF = BLOCK // 2
NEG = -1e30
FAR = 1 << 24
LOG2_SCALE = math.log2(math.e) / math.sqrt(HEAD_DIM)
BF = jnp.bfloat16
F32 = jnp.float32


VMEM_BYTES = 36 * 1024 * 1024
ANY = pl.BlockSpec(memory_space=pl.ANY)
PARAMS = pltpu.CompilerParams(vmem_limit_bytes=VMEM_BYTES)
TINY = pl.CostEstimate(flops=1, bytes_accessed=1, transcendentals=0)


def split_kv(info, keys, values):
    rows, half = keys.shape[0], keys.shape[1] // 2

    def kernel(info_ref, k_send, k_keep, v_send, v_keep, send_ref, keep_ref):
        send_ref[0], send_ref[1] = k_send[...], v_send[...]
        keep_ref[0], keep_ref[1] = k_keep[...], v_keep[...]

    there = pl.BlockSpec((rows, half), lambda i, info: (0, 1 - info[2]))
    here = pl.BlockSpec((rows, half), lambda i, info: (0, info[2]))
    whole = pl.BlockSpec((2, rows, half), lambda i, info: (0, 0, 0))
    shape = jax.ShapeDtypeStruct((2, rows, half), BF)
    return pl.pallas_call(
        kernel,
        grid_spec=pltpu.PrefetchScalarGridSpec(
            num_scalar_prefetch=1,
            grid=(1,),
            in_specs=[there, here, there, here],
            out_specs=(whole, whole),
        ),
        out_shape=(shape, shape),
        compiler_params=PARAMS,
        cost_estimate=TINY,
        name="split_kv",
    )(info, keys, keys, values, values)


def policy_terms(info, inputs, cotangent, after):
    rows, wide = inputs.shape
    half, step = cotangent.shape[1] // 2, 256

    def kernel(info_ref, in_ref, there_ref, here_ref, *refs):
        send_ref, keep_ref = refs[-2:]
        pos = info_ref[0] + lax.broadcasted_iota(jnp.int32, (rows, half), 0)
        for ref, out in ((there_ref, send_ref), (here_ref, keep_ref)):
            masked = jnp.where(pos < info_ref[1], ref[...], jnp.zeros((rows, half), BF))
            out[...] = lax.dot_general(
                in_ref[...], masked, (((0,), (0,)), ((), ())), preferred_element_type=F32
            ).astype(BF)

    out = pl.BlockSpec((step, half), lambda i, info: (i, 0))
    shape = jax.ShapeDtypeStruct((wide, half), BF)
    return pl.pallas_call(
        kernel,
        grid_spec=pltpu.PrefetchScalarGridSpec(
            num_scalar_prefetch=1,
            grid=(wide // step,),
            in_specs=[
                pl.BlockSpec((rows, step), lambda i, info: (0, i)),
                pl.BlockSpec((rows, half), lambda i, info: (0, 1 - info[2])),
                pl.BlockSpec((rows, half), lambda i, info: (0, info[2])),
            ]
            + [ANY] * len(after),
            out_specs=(out, out),
        ),
        out_shape=(shape, shape),
        compiler_params=PARAMS,
        cost_estimate=TINY,
        name="policy_terms",
    )(info, inputs, cotangent, cotangent, *after)


def combine(weights, terms, after):
    n, (rows, cols) = len(terms), terms[0].shape

    def kernel(w_ref, *refs):
        total = refs[0][...].astype(F32) * w_ref[0]
        for i in range(1, n):
            total += refs[i][...].astype(F32) * w_ref[i]
        refs[-1][...] = total.astype(BF)

    step = rows // 4
    spec = pl.BlockSpec((step, cols), lambda i, w: (i, 0))
    return pl.pallas_call(
        kernel,
        grid_spec=pltpu.PrefetchScalarGridSpec(
            num_scalar_prefetch=1,
            grid=(rows // step,),
            in_specs=[spec] * n + [ANY] * len(after),
            out_specs=spec,
        ),
        out_shape=jax.ShapeDtypeStruct((rows, cols), BF),
        compiler_params=PARAMS,
        cost_estimate=TINY,
        name="combine",
    )(weights, *terms, *after)


def place(info, pieces):
    n, (rows, cols) = len(pieces), pieces[0].shape
    chips = n // 2

    def kernel(info_ref, *refs):
        for i in range(n):

            @pl.when(pl.program_id(0) == i)
            def _():
                refs[n][...] = refs[i][...].astype(F32)

    return pl.pallas_call(
        kernel,
        grid_spec=pltpu.PrefetchScalarGridSpec(
            num_scalar_prefetch=1,
            grid=(n,),
            in_specs=[pl.BlockSpec((rows, cols), lambda i, info: (0, 0))] * n,
            out_specs=pl.BlockSpec(
                (rows, cols), lambda i, info: (info[i // 2], lax.rem(info[chips] + i, 2))
            ),
        ),
        out_shape=jax.ShapeDtypeStruct((chips * rows, 2 * cols), F32),
        compiler_params=PARAMS,
        cost_estimate=TINY,
        name="place",
    )(info, *pieces)


def add(info, sums, rows, steps, after):
    cols = sums[0][0][0].shape[1]
    counts = [len(terms) for terms in sums]
    n = sum(counts)

    def kernel(info_ref, *refs):
        start = 0
        for out, count in zip(refs[len(refs) - len(sums) :], counts):
            total = refs[start][...].astype(F32)
            for ref in refs[start + 1 : start + count]:
                total += ref[...].astype(F32)
            start += count
            out[...] = total.astype(BF)

    def spec(at):
        return pl.BlockSpec((rows, cols), lambda i, info: (at(i, info), 0))

    flat = [term for terms in sums for term in terms]
    shape = jax.ShapeDtypeStruct((rows * steps, cols), BF)
    return pl.pallas_call(
        kernel,
        grid_spec=pltpu.PrefetchScalarGridSpec(
            num_scalar_prefetch=1,
            grid=(steps,),
            in_specs=[spec(at) for _, at in flat] + [ANY] * len(after),
            out_specs=[spec(lambda i, info: i)] * len(sums),
        ),
        out_shape=[shape] * len(sums),
        compiler_params=PARAMS,
        cost_estimate=TINY,
        name="add",
    )(info, *(array for array, _ in flat), *after)


def pick(info, array, block, at, after):
    def kernel(info_ref, in_ref, *refs):
        refs[-1][...] = in_ref[...]

    zero = (0,) * len(block)
    return pl.pallas_call(
        kernel,
        grid_spec=pltpu.PrefetchScalarGridSpec(
            num_scalar_prefetch=1,
            grid=(1,),
            in_specs=[pl.BlockSpec(block, lambda i, info: at(info))] + [ANY] * len(after),
            out_specs=pl.BlockSpec(block, lambda i, info: zero),
        ),
        out_shape=jax.ShapeDtypeStruct(block, array.dtype),
        compiler_params=PARAMS,
        cost_estimate=TINY,
        name="pick",
    )(info, array, *after)


def in_hbm(array):
    return pltpu.with_memory_space_constraint(array, pltpu.HBM)


def attend(info, q, heads, pieces, joined, state, last, flops, after=()):
    n, n_after, first = len(pieces), len(after), not state
    wide = GROUP * HEAD_DIM

    def kernel(info_ref, here_ref, got_ref, *refs):
        kv_refs, refs = refs[: 2 * n], refs[2 * n :]
        if not first:
            acc_in, ml_in = refs[:2]
            refs = refs[2:]
        refs = refs[n_after:]
        out_a, out_b, q_s, k_s, v_s, acc_s, m_s = refs
        q_base, length, core = info_ref[0], info_ref[1], info_ref[2]
        for h in range(GROUP):
            cols = slice(h * HEAD_DIM, (h + 1) * HEAD_DIM)
            for part, ref in enumerate((here_ref, got_ref)):
                at = slice(part * HALF, (part + 1) * HALF)
                scaled = ref[:, cols].astype(F32) * LOG2_SCALE
                high = scaled.astype(BF)
                q_s[h, at, :HEAD_DIM] = high
                q_s[h, at, HEAD_DIM:] = (scaled - high.astype(F32)).astype(BF)
            if first:
                acc_s[h] = jnp.zeros((BLOCK, 2 * HEAD_DIM), F32)
                m_s[h] = jnp.full((BLOCK, HEAD_DIM), NEG, F32)
            else:
                acc_s[h, :, :HEAD_DIM] = acc_in[0, :, cols]
                m_s[h] = jnp.broadcast_to(ml_in[0, :, h : h + 1], (BLOCK, HEAD_DIM))
                acc_s[h, :, HEAD_DIM:] = jnp.broadcast_to(
                    ml_in[0, :, 8 + h : 9 + h], (BLOCK, HEAD_DIM)
                )
        for i in range(n):
            at = slice(i * BLOCK, (i + 1) * BLOCK)
            k_s[at, :HEAD_DIM] = kv_refs[2 * i][0]
            k_s[at, HEAD_DIM:] = kv_refs[2 * i][0]
            v_s[at, :HEAD_DIM] = kv_refs[2 * i + 1][0]
            v_s[at, HEAD_DIM:] = jnp.ones((BLOCK, HEAD_DIM), BF)

        def tiles(i, count, keep):
            keys = count * BLOCK
            at = pl.ds(pl.multiple_of(i * BLOCK, BLOCK), keys)
            kk, v1 = k_s[at, :], v_s[at, :]

            def scores(h):
                s = lax.dot_general(
                    q_s[h], kk, (((1,), (1,)), ((), ())), preferred_element_type=F32
                )
                return s if keep is None else jnp.where(keep, s, NEG)

            s = scores(0)
            for h in range(GROUP):
                later = scores(h + 1) if h + 1 < GROUP else None
                m_old = m_s[h]
                m_new = jnp.maximum(m_old, jnp.max(s, axis=1, keepdims=True))
                p = jnp.exp2(s - jnp.tile(m_new, (1, keys // HEAD_DIM)))
                pv = jnp.dot(p.astype(BF), v1, preferred_element_type=F32)
                m_s[h] = m_new
                acc_s[h] = acc_s[h] * jnp.tile(jnp.exp2(m_old - m_new), (1, 2)) + pv
                s = later

        taken = []
        for begin, count in joined:
            far = info_ref[3 + begin]
            for i in range(begin + 1, begin + count):
                far = jnp.maximum(far, info_ref[3 + i])
            together = (far < q_base) & (far + BLOCK <= length)
            taken.append((begin, count, together))

            @pl.when(together)
            def _():
                tiles(begin, count, None)

        @pl.loop(0, n)
        def _(i):
            base = info_ref[3 + i]
            use = (base <= q_base) & (base < length)
            for begin, count, together in taken:
                use &= jnp.logical_not(together & (i >= begin) & (i < begin + count))

            @pl.when(use)
            def _():
                row = lax.broadcasted_iota(jnp.int32, (BLOCK, BLOCK), 0)
                col = lax.broadcasted_iota(jnp.int32, (BLOCK, BLOCK), 1)
                row = q_base + ((row + HALF * core) & (BLOCK - 1))
                col = base + ((col + HALF * core) & (BLOCK - 1))
                tiles(i, 1, (col <= row) & (col < length))

        if last:
            for h in range(GROUP):
                cols = slice(h * HEAD_DIM, (h + 1) * HEAD_DIM)
                mixed = (acc_s[h, :, :HEAD_DIM] / acc_s[h, :, HEAD_DIM:]).astype(BF)
                out_a[:, cols] = mixed[:HALF]
                out_b[:, cols] = mixed[HALF:]
        else:
            lane = lax.broadcasted_iota(jnp.int32, (BLOCK, HEAD_DIM), 1)
            ml = jnp.zeros((BLOCK, HEAD_DIM), F32)
            for h in range(GROUP):
                out_a[0, :, h * HEAD_DIM : (h + 1) * HEAD_DIM] = acc_s[h, :, :HEAD_DIM]
                ml = jnp.where(lane == h, m_s[h], ml)
                ml = jnp.where(lane == 8 + h, acc_s[h, :, HEAD_DIM:], ml)
            out_b[0] = ml

    def kv_spec(index):
        return pl.BlockSpec((1, BLOCK, HEAD_DIM), lambda g, info: (index, 0, g))

    operands, kv_specs = [], []
    for kv in pieces:
        operands += [in_hbm(kv)] * 2
        kv_specs += [kv_spec(0), kv_spec(1)]
    q_specs = [
        pl.BlockSpec((HALF, wide), lambda g, info: (0, info[2] * heads + g)),
        pl.BlockSpec((HALF, wide), lambda g, info: (0, g)),
    ]
    out_spec = pl.BlockSpec((HALF, wide), lambda g, info: (0, g))
    acc_spec = pl.BlockSpec((1, BLOCK, wide), lambda g, info: (g, 0, 0))
    ml_spec = pl.BlockSpec((1, BLOCK, HEAD_DIM), lambda g, info: (g, 0, 0))
    acc_shape = pltpu.HBM((heads, BLOCK, wide), F32)
    ml_shape = pltpu.HBM((heads, BLOCK, HEAD_DIM), F32)
    out_shape = jax.ShapeDtypeStruct((HALF, heads * wide), BF)
    return pl.pallas_call(
        kernel,
        grid_spec=pltpu.PrefetchScalarGridSpec(
            num_scalar_prefetch=1,
            grid=(heads,),
            in_specs=q_specs
            + kv_specs
            + ([] if first else [acc_spec, ml_spec])
            + [ANY] * n_after,
            out_specs=(out_spec, out_spec) if last else (acc_spec, ml_spec),
            scratch_shapes=[
                pltpu.VMEM((GROUP, BLOCK, 2 * HEAD_DIM), BF),
                pltpu.VMEM((n * BLOCK, 2 * HEAD_DIM), BF),
                pltpu.VMEM((n * BLOCK, 2 * HEAD_DIM), BF),
                pltpu.VMEM((GROUP, BLOCK, 2 * HEAD_DIM), F32),
                pltpu.VMEM((GROUP, BLOCK, HEAD_DIM), F32),
            ],
        ),
        out_shape=(out_shape, out_shape) if last else (acc_shape, ml_shape),
        compiler_params=PARAMS,
        cost_estimate=pl.CostEstimate(
            flops=flops, bytes_accessed=1, transcendentals=0
        ),
        name="attend",
    )(info, *(in_hbm(a) for a in q), *operands, *(in_hbm(a) for a in state), *after)


def finish(info, own, other, gain, head, after):
    rows, half = own.shape

    def kernel(info_ref, own_ref, other_ref, gain_ref, head_ref, *refs):
        out_ref, sum_ref = refs[-2:]
        base, length, core = info_ref[0], info_ref[1], info_ref[2]
        squares = jnp.zeros((rows, 1), F32)
        score = jnp.zeros((rows, 1), F32)
        for ref, side in ((own_ref, core), (other_ref, 1 - core)):
            cols = pl.ds(pl.multiple_of(side * half, half), half)
            part = ref[...]
            out_ref[:, cols] = part
            part = part.astype(F32)
            squares += jnp.sum(part * part, axis=1, keepdims=True)
            score += jnp.sum(part * (gain_ref[:, cols] * head_ref[:, cols]), axis=1, keepdims=True)
        score = score * lax.rsqrt(squares / (2 * half) + 1e-6)
        pos = base + lax.broadcasted_iota(jnp.int32, (rows, 1), 0)
        score = jnp.where(pos < length, score, 0.0)
        sum_ref[...] = jnp.broadcast_to(jnp.sum(score, axis=0, keepdims=True), (8, HEAD_DIM))

    return pl.pallas_call(
        kernel,
        grid_spec=pltpu.PrefetchScalarGridSpec(
            num_scalar_prefetch=1,
            grid=(1,),
            in_specs=[
                pl.BlockSpec((rows, half), lambda g, _: (0, 0)),
                pl.BlockSpec((rows, half), lambda g, _: (0, 0)),
                pl.BlockSpec((1, 2 * half), lambda g, _: (0, 0)),
                pl.BlockSpec((1, 2 * half), lambda g, _: (0, 0)),
            ]
            + [ANY] * len(after),
            out_specs=(
                pl.BlockSpec((rows, 2 * half), lambda g, _: (0, 0)),
                pl.BlockSpec((8, HEAD_DIM), lambda g, _: (0, 0)),
            ),
        ),
        out_shape=(
            jax.ShapeDtypeStruct((rows, 2 * half), BF),
            jax.ShapeDtypeStruct((8, HEAD_DIM), F32),
        ),
        compiler_params=PARAMS,
        cost_estimate=TINY,
        name="finish",
    )(info, own, other, gain[None], head[None], *after)


def shards(
    queries, keys, values, valid_length, norm_gain, value_head, policy_in, cotangent, qkv_weight
):
    n_rep, n_fsdp, n_ctx = (lax.axis_size(a) for a in ("replica", "fsdp", "context"))
    n_x, n_z = n_ctx // 2, n_rep // 2
    f, ctx, rep = lax.axis_index("fsdp"), lax.axis_index("context"), lax.axis_index("replica")
    x, core = ctx // 2, ctx % 2
    length = valid_length[0]
    rows = queries.shape[1]

    swap = [(i, i ^ 1) for i in range(n_ctx)]

    def along_x(step, planes):
        return [
            (p * n_ctx + i, p * n_ctx + (i + 2 * step) % n_ctx)
            for p in planes
            for i in range(n_ctx)
        ]

    def move(array, step, planes):
        return lax.ppermute(array, ("fsdp", "context"), along_x(step, planes))

    def side(array, which, axis):
        size = array.shape[axis] // 2
        return lax.dynamic_slice_in_dim(array, which * size, size, axis)

    tok_base = (f * n_ctx + ctx) * rows
    tok_info = jnp.stack([tok_base, length, core, f, x]).astype(jnp.int32)

    tok_base = (f * n_ctx + ctx) * rows
    tok_info = jnp.stack([tok_base, length, core, f, x]).astype(jnp.int32)
    kv_heads = keys.shape[2] // HEAD_DIM // 2

    kv_send, kv_keep = split_kv(tok_info, keys[0], values[0])
    kv_own = jnp.concatenate([kv_keep, lax.ppermute(kv_send, "context", swap)], axis=1)
    p_send, p_keep = policy_terms(tok_info, policy_in[0], cotangent[0], (kv_keep,))
    q_here = queries[0]
    q_send = pick(
        tok_info, q_here, (rows, q_here.shape[1] // 2), lambda info: (0, 1 - info[2]), (p_send,)
    )
    q_got = lax.ppermute(q_send, "context", swap)

    both, later = range(n_fsdp), [1]
    cross = {0: lax.ppermute(kv_own, "fsdp", [(0, 1)])}
    ring = {d: move(kv_own, d, both) for d in (1, 3, 2)}
    for d in (1, 3, 2):
        cross[d] = move(cross[0], d, later)

    pairs = []
    for r in range(n_rep):
        for g in range(n_fsdp):
            y_to = ((r % 2) * 2 + g) ^ 3
            pairs.append((r * 2 + g, ((r // 2) * 2 + y_to // 2) * 2 + y_to % 2))
    weight_other = lax.ppermute(qkv_weight, ("replica", "fsdp"), pairs)

    def pos(plane, d):
        return (plane * n_x + (x - d) % n_x) * BLOCK

    def near(*distances):
        return [pos(f, d) for d in distances]

    def other(*distances):
        return [jnp.where(f == 1, pos(0, d), FAR) for d in distances]

    def step(positions, pieces, joined, state, flops, after):
        items = [pos(f, 0), length, core] + positions
        info = jnp.stack([jnp.asarray(i, jnp.int32) for i in items])
        return attend(info, (q_here, q_got), kv_heads, pieces, joined, state, bool(state), flops, after)

    chunk = p_keep.shape[0] // (n_fsdp * n_x)
    got = lax.ppermute(p_send, "context", swap)
    p_send, p_keep = add(
        tok_info,
        [
            [(a, lambda i, info: (1 - info[3]) * n_x + i) for a in (p_keep, got)],
            [(a, lambda i, info: info[3] * n_x + i) for a in (p_keep, got)],
        ],
        chunk,
        n_x,
        (cross[0],),
    )
    got = lax.ppermute(p_send, "fsdp", [(0, 1), (1, 0)])

    valid = tok_base + jnp.arange(rows, dtype=jnp.int32) < length
    masked = jnp.where(valid[:, None], cotangent[0], jnp.zeros_like(cotangent[0]))

    def raw(weight):
        return lax.dot_general(
            masked, weight, (((1,), (1,)), ((), ())), preferred_element_type=F32
        )

    raw_own = raw(qkv_weight)

    state = step(
        other(0) + near(1, 3, 2, 0),
        [cross[0], ring[1], ring[3], ring[2], kv_own],
        [(0, 2), (2, 2)],
        (),
        flops=24 * 10**9,
        after=(p_send, raw_own),
    )
    chunks = add(
        tok_info,
        [
            [(a, lambda i, info, d=d: lax.rem(info[4] + d, n_x)) for a in (p_keep, got)]
            for d in range(n_x)
        ],
        chunk,
        1,
        state[1:],
    )
    parts = [chunks[0]] + [move(chunks[d], d, both) for d in range(1, n_x)]
    mixed = step(
        other(1, 3, 2),
        [cross[1], cross[3], cross[2]],
        [(0, 3)],
        state,
        flops=24 * 10**9,
        after=(chunks[0],),
    )
    (total,) = add(tok_info, [[(a, lambda i, info: 0) for a in parts]], chunk, 1, mixed[:1])
    mixed_there = pick(tok_info, mixed[1], mixed[1].shape, lambda info: (0, 0), (total,))

    z, y_hi = rep // 2, rep % 2

    def along_z(array, dz):
        pairs = [(r, (r + 2 * dz) % n_rep) for r in range(n_rep)]
        return lax.ppermute(array, "replica", pairs) if dz else array

    terms = [along_z(total, dz) for dz in range(n_z)]
    sources = jnp.stack([((z - dz) % n_z) * 2 + y_hi for dz in range(n_z)])
    attn_out, reward_sum = finish(
        tok_info,
        mixed[0],
        lax.ppermute(mixed_there, "context", swap),
        norm_gain,
        value_head,
        (weight_other,),
    )

    raw_other = raw(weight_other)

    partial = reward_sum[:1] / jnp.sqrt(length.astype(F32))
    n_dev = n_rep * n_fsdp * n_ctx
    sums = lax.all_to_all(
        jnp.broadcast_to(partial, (n_dev, HEAD_DIM)),
        ("replica", "fsdp", "context"),
        0,
        0,
        tiled=True,
    )
    reward = jnp.sum(sums[:, 0].reshape(n_rep, n_fsdp * n_ctx), axis=1)
    mean = jnp.mean(reward)
    var = jnp.mean(reward * reward) - mean * mean
    advantages = (reward - mean) / jnp.sqrt(var + 0.25)
    advantage = lax.dynamic_slice_in_dim(advantages, rep, 1)

    weight_rows = combine(advantages[sources], terms, (raw_own, raw_other))
    beside = lax.ppermute(weight_rows, "replica", [(r, r ^ 1) for r in range(n_rep)])
    (weight_rows,) = add(
        tok_info, [[(a, lambda i, info: 0) for a in (weight_rows, beside)]], chunk, 1, ()
    )
    parts = []
    for d in (0, 1, 3, 2):
        part = move(weight_rows, d, both) if d else weight_rows
        parts += [part, lax.ppermute(part, "context", swap)]
    chips = [(x - d) % n_x for d in (0, 1, 3, 2)]
    weight_grad = place(jnp.stack(chips + [core]).astype(jnp.int32), parts)
    input_grad = jnp.where(
        f == 0,
        jnp.concatenate([raw_own, raw_other], axis=1),
        jnp.concatenate([raw_other, raw_own], axis=1),
    )
    input_grad = (advantage * input_grad).astype(BF)
    return (attn_out[None], advantage, input_grad[None], weight_grad)


def solution(mesh):
    tokens = P("replica", ("fsdp", "context"), None)
    in_specs = (tokens, tokens, tokens, P("replica"), P(), P(), tokens, tokens, P("fsdp", None))
    out_specs = (tokens, P("replica"), tokens, P("fsdp", None))
    return jax.shard_map(shards, mesh=mesh, in_specs=in_specs, out_specs=out_specs, check_vma=False)
```
